32 devices in a mesh: section: 2 (over x), expert: 4 (over z), tensor: 4 (over y, core).
Axes of the slice: x: 2, y: 2, z: 4, core: 2. Of those that a mesh axis runs over, the one named last changes fastest.
Arguments:
- slab: bfloat16 [2, 768, 7168], P('section', ('expert', 'tensor')), may hold values from -6 to 6
- route_ids: int32 [2, 768, 2], P('section', ('expert', 'tensor')), may hold values from 0 to 3, all different within a row; in each aligned block of 48 rows (0 to 47, 48 to 95, ..., all dimensions but the last counted through in order) at most 48 rows name the same one
- route_weights: float32 [2, 768, 2], P('section', ('expert', 'tensor')), may hold values from 0.1 to 1
- norm_gain: float32 [2, 7168], P('section'), may hold values from 0.25 to 1.75
- w_gate: bfloat16 [2, 4, 7168, 1024], P('section', 'expert', None, 'tensor'), may hold values from -0.0625 to 0.0625
- w_up: bfloat16 [2, 4, 7168, 1024], P('section', 'expert', None, 'tensor'), may hold values from -0.0625 to 0.0625
- w_down: bfloat16 [2, 4, 1024, 7168], P('section', 'expert', 'tensor'), may hold values from -0.1875 to 0.1875
Outputs:
- next_slab: bfloat16 [2, 768, 7168], P('section', ('expert', 'tensor'))
The draws below stay inside these ranges and needn't reach their ends.
Inputs may be any that keep to these rules, and one draw needn't show every extreme that they name: `route_ids`: within the rows of one device (aligned blocks of 48 token rows) no expert is named by more than 48 rows, a bound that some block reaches. The ids of a row differ.
All inputs are finite; a program needn't handle non-finite values.
Results may differ from the reference program's by a relative error of at most 0.006.
Values may be sent and summed in bfloat16 or wider, within the bound.
A program may use at most 128 MiB of HBM per device.

```python
import math
import jax
import jax.numpy as jnp
import numpy as np
from jax import lax

D = 7168
FF = 1024
TOPK = 2
TOK_DEV = 48
EXPERTS = 4
FFD = 256
CAP = 48
TOKENS = 768
N_SECTION = 2
N_EXPERT = 4
N_TENSOR = 4


def steps_of(stream_key, dims, pieces, smallest, high):
    def one(position, blocks):
        draws = jax.random.uniform(jax.random.fold_in(jax.random.fold_in(stream_key, 6), position), (blocks,), jnp.float32, smallest / len(pieces), high / len(pieces))
        return jnp.repeat(jnp.exp(draws), dims[position] // blocks).reshape((-1,) + (1,) * (len(dims) - position - 1))

    level = one(*pieces[0])
    for cut in pieces[1:]:
        level = level * one(*cut)
    return level


def assign_block(rng, own, number, rows, count, top, bound, skew):
    ranking = jax.random.permutation(rng, count)
    heavy_load, common = portions_of(count, rows * top, bound, skew, True), portions_of(count, rows * top, bound, skew, False)
    places = jnp.arange(count)

    def named(sizes, rotation):
        used = int((sizes > 0).sum())
        fixed = max(1, used // 4)
        moved = fixed + (places - fixed + rotation * (used - fixed)) % max(1, count - fixed)
        return jnp.zeros((count,), jnp.int32).at[ranking[jnp.where(places < fixed, places, moved)]].set(jnp.asarray(sizes, jnp.int32))

    sizes = jnp.where(number % 4 == 0, named(heavy_load, number // 4), named(common, number - number // 4 - 1))
    mixed = jax.random.permutation(jax.random.fold_in(own, 3), count)
    source_of, receiver = mixed[0:count // 2 * 2:2], mixed[1:count // 2 * 2:2]
    room = jnp.minimum(sizes[source_of] - 1, bound - sizes[receiver]) // 2
    room = jnp.where((source_of == ranking[0]) | (receiver == ranking[0]) | (sizes[receiver] == 0), 0, jnp.maximum(room, 0))
    moved = jax.random.randint(jax.random.fold_in(own, 4), (count // 2,), 0, 1 << 20) % (room + 1)
    sizes = sizes.at[source_of].add(-moved).at[receiver].add(moved)
    labels = jnp.searchsorted(jnp.cumsum(sizes), jnp.arange(rows * top), side="right").astype(jnp.int32)
    table = labels.reshape(top, rows).T
    table = table[jax.random.permutation(jax.random.fold_in(own, 1), rows)]
    rotation = jax.random.randint(jax.random.fold_in(own, 2), (rows, 1), 0, top)
    return jnp.take_along_axis(table, (jnp.arange(top)[None, :] + rotation) % top, axis=1)


def portions_of(amount, total, reach, slope, full):
    weights = [(1 << 20) // math.isqrt(standing ** slope) + 1 for standing in range(1, amount + 1)]
    largest = reach if full else min(reach, max(-(-total // amount), total * weights[0] // sum(weights)))
    least = 1 if total - largest >= amount - 1 else 0
    holding, spare = [largest] + [least] * (amount - 1), total - largest - least * (amount - 1)
    while spare > 0:
        movable = [i for i in range(1, amount) if holding[i] < largest] or [i for i in range(1, amount) if holding[i] < reach]
        pool, left = sum([weights[i] for i in movable]), spare
        for i in movable:
            addition = min(reach - holding[i], max(1, left * weights[i] // pool), spare)
            holding[i] = holding[i] + addition
            spare = spare - addition
    return np.array(holding)


def noise(rng, dims, scale, limit, pieces=(), kind=jnp.bfloat16):
    result = scale * jax.random.normal(rng, dims, jnp.float32)
    if pieces:
        result = result * steps_of(rng, dims, pieces, -0.22, 0.18)
    return jnp.clip(result, -limit, limit).astype(kind)


def setup_inputs(seed: int = 0) -> dict:
    key_list = jax.random.split(jax.random.key(seed), 8)
    slab = noise(key_list[0], (N_SECTION, TOKENS, D), 1.0, 6.0, ((0, 2), (1, 16)))
    route_ids_keys = jax.random.split(jax.random.fold_in(key_list[1], 1), N_SECTION * TOKENS // TOK_DEV)
    route_ids_turns = jax.random.permutation(jax.random.fold_in(key_list[1], 3), N_SECTION * TOKENS // TOK_DEV)
    route_ids = jax.vmap(lambda own, number: assign_block(jax.random.fold_in(key_list[1], 2), own, number, TOK_DEV, EXPERTS, TOPK, CAP, 2))(route_ids_keys, route_ids_turns).reshape((N_SECTION, TOKENS, TOPK))
    route_weights = jnp.clip(0.1 + 0.9 * jax.random.uniform(key_list[2], (N_SECTION, TOKENS, TOPK), jnp.float32) ** steps_of(key_list[2], (N_SECTION, TOKENS, TOPK), ((0, 2), (1, 16)), -0.2, 0.2), 0.1, 1.0)
    norm_gain = jnp.clip(1.0 + 0.15 * jax.random.normal(key_list[3], (N_SECTION, D), jnp.float32), 0.25, 1.75)
    w_gate = noise(key_list[4], (N_SECTION, EXPERTS, D, FF), D ** -0.5, 0.0625, ((0, 2), (1, 4), (3, 4)))
    w_up = noise(key_list[5], (N_SECTION, EXPERTS, D, FF), D ** -0.5, 0.0625, ((0, 2), (1, 4), (3, 4)))
    w_down = noise(key_list[6], (N_SECTION, EXPERTS, FF, D), FF ** -0.5, 0.1875, ((0, 2), (1, 4), (2, 4)))
    return dict(slab=slab, route_ids=route_ids, route_weights=route_weights, norm_gain=norm_gain, w_gate=w_gate, w_up=w_up, w_down=w_down)


def rms_normed(rows, gain):
    values = rows.astype(jnp.float32)
    scale = lax.rsqrt(lax.optimization_barrier(jnp.mean(values * values, axis=-1, keepdims=True)) + 1e-06)
    return (values * scale * gain.astype(jnp.float32)).astype(jnp.bfloat16)

def expert_apply(rows, gate_w, up_w, down_w):
    gate = jnp.dot(rows, gate_w, preferred_element_type=jnp.float32)
    up = jnp.dot(rows, up_w, preferred_element_type=jnp.float32)
    hidden = (jax.nn.silu(gate) * up).astype(jnp.bfloat16)
    count = rows.shape[0]
    slices = hidden.reshape(count, N_TENSOR, FFD).astype(jnp.float32)
    down_parts = down_w.reshape(N_TENSOR, FFD, D).astype(jnp.float32)
    parts = jnp.einsum('mqf,qfd->qmd', slices, down_parts)
    rounded = lax.optimization_barrier(parts.astype(jnp.bfloat16))
    return lax.optimization_barrier(jnp.sum(rounded.astype(jnp.float32), axis=0)).astype(jnp.bfloat16)

def reference(slab, route_ids, route_weights, norm_gain, w_gate, w_up, w_down):
    arriving = jnp.roll(slab, 1, axis=0)
    padded_rows = N_EXPERT * N_TENSOR * CAP
    results = []
    for section in range(N_SECTION):
        rows = arriving[section]
        normed = rms_normed(rows, norm_gain[section])
        ids = route_ids[section].reshape(-1).astype(jnp.int32)
        count = ids.shape[0]
        onehot = (ids[:, None] == jnp.arange(EXPERTS, dtype=jnp.int32)[None, :]).astype(jnp.int32)
        rank = lax.optimization_barrier(jnp.sum((jnp.cumsum(onehot, axis=0) - onehot) * onehot, axis=1)).astype(jnp.int32)
        table = jnp.zeros((EXPERTS, padded_rows), jnp.int32)
        table = table.at[ids, rank].set(jnp.arange(count, dtype=jnp.int32) // TOPK)

        def one_expert(items):
            index_row, gate_w, up_w, down_w = items
            return expert_apply(normed[index_row], gate_w, up_w, down_w)
        outputs = lax.map(one_expert, (table, w_gate[section], w_up[section], w_down[section]))
        picked = outputs[ids, rank].astype(jnp.float32)
        weighted = picked * route_weights[section].reshape(-1)[:, None].astype(jnp.float32)
        mixed = lax.optimization_barrier(jnp.sum(weighted.reshape(TOKENS, TOPK, D), axis=1))
        results.append((rows.astype(jnp.float32) + mixed).astype(jnp.bfloat16))
    return jnp.stack(results, axis=0)
```

```python
import functools

import jax
import jax.numpy as jnp
from jax import lax
from jax.experimental import pallas as pl
from jax.experimental.pallas import tpu as pltpu
from jax.sharding import PartitionSpec as P

MESH = pl.DeviceIdType.MESH
CHUNK = 16
PAD = 128
CORES = 2


def kernel(
    sizes,
    slab_ref,
    ids_ref,
    rw_ref,
    gain_ref,
    wg_ref,
    wu_ref,
    wd_ref,
    out_ref,
    xbuf,
    tok,
    wgs,
    wus,
    wds,
    hid,
    part,
    yrecv,
    zrecv,
    x_send,
    x_recv,
    w_local,
    w_send,
    w_recv,
    t_right,
    t_left,
    t_y,
    t_recv,
    p_y,
    p_yrecv,
    p_z,
    p_zrecv,
):
    sections, owners, groups = sizes
    rows, width = out_ref.shape
    chunks = rows // CHUNK
    section = lax.axis_index("section")
    z = lax.axis_index("expert")
    t = lax.axis_index("tensor")
    core = lax.rem(t, CORES)
    y = t // CORES
    other_y = 1 - y
    mate = {"tensor": y * CORES + 1 - core}
    across = {"tensor": other_y * CORES + core}
    ahead = {"section": lax.rem(section + 1, sections)}
    behind = {"section": lax.rem(section + sections - 1, sections)}
    right = {"expert": lax.rem(z + 1, owners)}
    left = {"expert": lax.rem(z + owners - 1, owners)}
    has_right = z < owners - 1
    has_left = z > 0

    def remote(src, dst, send, recv, where):
        return pltpu.make_async_remote_copy(
            src_ref=src,
            dst_ref=dst,
            send_sem=send,
            recv_sem=recv,
            device_id=where,
            device_id_type=MESH,
        )

    def lines(k, side=None):
        if side is None:
            return pl.ds(k * CHUNK, CHUNK)
        return pl.ds(pl.multiple_of(side * rows + k * CHUNK, CHUNK), CHUNK)

    barrier = pltpu.get_barrier_semaphore()
    for where in (mate, across, ahead, behind):
        pl.semaphore_signal(barrier, inc=1, device_id=where, device_id_type=MESH)

    @pl.when(has_right)
    def _():
        pl.semaphore_signal(barrier, inc=1, device_id=right, device_id_type=MESH)

    @pl.when(has_left)
    def _():
        pl.semaphore_signal(barrier, inc=1, device_id=left, device_id_type=MESH)

    edge = jnp.where(has_right, 1, 0) + jnp.where(has_left, 1, 0)
    pl.semaphore_wait(barrier, 4 + edge)

    def x_copy(k):
        return remote(
            slab_ref.at[lines(k)], xbuf.at[lines(k)], x_send.at[k], x_recv.at[k], ahead
        )

    for k in range(chunks):
        x_copy(k).start()

    weights = ((wg_ref, wgs), (wu_ref, wus), (wd_ref, wds))

    def w_copies(i):
        source, target = weights[i]
        return (
            pltpu.make_async_copy(source, target.at[core], w_local.at[i]),
            remote(source, target.at[core], w_send.at[i], w_recv.at[i], mate),
        )

    for i in range(3):
        for copy in w_copies(i):
            copy.start()

    def t_copy(zs, k, sends, where):
        place = tok.at[zs, lines(k, y)]
        return remote(place, place, sends.at[zs, k], t_recv.at[y, zs, k], where)

    def t_arrived(zs, side, k):
        place = tok.at[zs, lines(k, side)]
        return remote(place, place, t_y.at[zs, k], t_recv.at[side, zs, k], across)

    lane = lax.broadcasted_iota(jnp.int32, (CHUNK, PAD), 1)
    for k in range(chunks):
        x_copy(k).wait_recv()
        values = xbuf[lines(k)].astype(jnp.float32)
        scale = lax.rsqrt(jnp.mean(values * values, axis=-1, keepdims=True) + 1e-06)
        tok[z, lines(k, y), 0:width] = (values * scale * gain_ref[...]).astype(
            jnp.bfloat16
        )
        expert = lax.rem(lane, owners)
        dense = jnp.zeros((CHUNK, PAD), jnp.float32)
        for c in range(ids_ref.shape[1]):
            hit = expert == ids_ref[lines(k), c : c + 1]
            dense = jnp.where(hit, rw_ref[lines(k), c : c + 1], dense)
        high = dense.astype(jnp.bfloat16).astype(jnp.float32)
        rest = dense - high
        middle = rest.astype(jnp.bfloat16).astype(jnp.float32)
        low = rest - middle
        third = lane // owners
        packed = jnp.where(
            third == 0,
            high,
            jnp.where(third == 1, middle, jnp.where(third == 2, low, 0.0)),
        )
        tok[z, lines(k, y), width : width + PAD] = packed.astype(jnp.bfloat16)

        @pl.when(has_right)
        def _():
            t_copy(z, k, t_right, right).start()

        @pl.when(has_left)
        def _():
            t_copy(z, k, t_left, left).start()

        t_copy(z, k, t_y, across).start()

    def at(j):
        return z + ((j + 1) // 2) * (1 - 2 * lax.rem(j, 2))

    def inside(zs):
        return jnp.logical_and(zs >= 0, zs < owners)

    def forward(zs):
        for k in range(chunks):
            t_arrived(zs, y, k).wait_recv()

            @pl.when(jnp.logical_and(zs < z, has_right))
            def _():
                t_copy(zs, k, t_right, right).start()

            @pl.when(jnp.logical_and(zs > z, has_left))
            def _():
                t_copy(zs, k, t_left, left).start()

            t_copy(zs, k, t_y, across).start()

    tall = 2 * rows
    hidden_width = wgs.shape[2]
    tile = width // 7 if width % (7 * 128) == 0 else 128

    def compute(zs):
        for k in range(chunks):
            t_arrived(zs, other_y, k).wait_recv()
        for h in range(CORES):
            gate = jnp.dot(
                tok[zs, :, 0:width], wgs[h], preferred_element_type=jnp.float32
            )
            up = jnp.dot(
                tok[zs, :, 0:width], wus[h], preferred_element_type=jnp.float32
            )
            hid[:, h * hidden_width : (h + 1) * hidden_width] = (
                jax.nn.silu(gate) * up
            ).astype(jnp.bfloat16)
        spot = lax.broadcasted_iota(jnp.int32, (tall, PAD), 1)
        mine = jnp.logical_and(lax.rem(spot, owners) == z, spot < 3 * owners)
        share = jnp.sum(
            jnp.where(mine, tok[zs, :, width : width + PAD].astype(jnp.float32), 0.0),
            axis=1,
            keepdims=True,
        )

        def down(i, carry):
            span = pl.ds(pl.multiple_of(i * tile, 128), tile)
            product = jnp.dot(
                hid[:, 0:hidden_width],
                wds[0, :, span],
                preferred_element_type=jnp.float32,
            ) + jnp.dot(
                hid[:, hidden_width : 2 * hidden_width],
                wds[1, :, span],
                preferred_element_type=jnp.float32,
            )
            part[zs, :, span] = (product * share).astype(jnp.bfloat16)
            return carry

        lax.fori_loop(0, width // tile, down, 0)

    def gather_step(j, carry):
        zs = at(j)

        @pl.when(jnp.logical_and(j < 2 * owners - 1, inside(zs)))
        def _():
            forward(zs)

        before = at(j - 2)

        @pl.when(j == 2)
        def _():
            for i in range(3):
                local_copy, mate_copy = w_copies(i)
                local_copy.wait()
                remote(
                    weights[i][0],
                    weights[i][1].at[1 - core],
                    w_send.at[i],
                    w_recv.at[i],
                    mate,
                ).wait_recv()

        @pl.when(jnp.logical_and(j >= 2, inside(before)))
        def _():
            compute(before)

        return carry

    lax.fori_loop(1, 2 * owners + 1, gather_step, 0)

    def y_copy(zs, k):
        return remote(
            part.at[zs, lines(k, other_y)],
            yrecv.at[zs, lines(k)],
            p_y.at[zs, k],
            p_yrecv.at[zs, k],
            across,
        )

    def z_copy(zs, slot, k, where):
        return remote(
            part.at[zs, lines(k, y)],
            zrecv.at[slot, lines(k)],
            p_z.at[zs, k],
            p_zrecv.at[slot, k],
            where,
        )

    def send_y(i, carry):
        zs = at(2 * owners - 2 - i)

        @pl.when(inside(zs))
        def _():
            for k in range(chunks):
                y_copy(zs, k).start()

        return carry

    lax.fori_loop(0, 2 * owners - 1, send_y, 0)

    def reduce_step(i, carry):
        zs = at(2 * owners - 2 - i)

        @pl.when(inside(zs))
        def _():
            for k in range(chunks):
                y_copy(zs, k).wait_recv()
                where = (zs, lines(k, y))
                both = part[where].astype(jnp.float32) + yrecv[zs, lines(k)].astype(
                    jnp.float32
                )
                outer = jnp.logical_or(
                    jnp.logical_and(zs > z, has_left),
                    jnp.logical_and(zs < z, has_right),
                )

                @pl.when(outer)
                def _():
                    z_copy(zs, zs, k, right).wait_recv()
                    part[where] = (
                        both + zrecv[zs, lines(k)].astype(jnp.float32)
                    ).astype(jnp.bfloat16)

                @pl.when(jnp.logical_not(outer))
                def _():
                    part[where] = both.astype(jnp.bfloat16)

                @pl.when(zs > z)
                def _():
                    z_copy(zs, zs, k, right).start()

                @pl.when(zs < z)
                def _():
                    slot = jnp.where(zs == z - 1, owners, zs)
                    z_copy(zs, slot, k, left).start()

        return carry

    lax.fori_loop(0, 2 * owners - 2, reduce_step, 0)

    for k in range(chunks):
        y_copy(z, k).wait_recv()
        total = (
            xbuf[lines(k)].astype(jnp.float32)
            + part[z, lines(k, y)].astype(jnp.float32)
            + yrecv[z, lines(k)].astype(jnp.float32)
        )
        hid_zero = jnp.zeros((CHUNK, width), jnp.bfloat16)

        @pl.when(has_left)
        def _():
            z_copy(z, z, k, right).wait_recv()

        @pl.when(jnp.logical_not(has_left))
        def _():
            zrecv[z, lines(k)] = hid_zero

        @pl.when(has_right)
        def _():
            z_copy(z, owners, k, left).wait_recv()

        @pl.when(jnp.logical_not(has_right))
        def _():
            zrecv[owners, lines(k)] = hid_zero

        total = total + (
            zrecv[z, lines(k)].astype(jnp.float32)
            + zrecv[owners, lines(k)].astype(jnp.float32)
        )
        out_ref[lines(k)] = total.astype(jnp.bfloat16)

    for k in range(chunks):
        x_copy(k).wait_send()
    for i in range(3):
        w_copies(i)[1].wait_send()

    def settle(zs, carry):
        for k in range(chunks):
            t_copy(zs, k, t_y, across).wait_send()
            y_copy(zs, k).wait_send()

            @pl.when(jnp.logical_and(zs <= z, has_right))
            def _():
                t_copy(zs, k, t_right, right).wait_send()

            @pl.when(jnp.logical_and(zs >= z, has_left))
            def _():
                t_copy(zs, k, t_left, left).wait_send()

            @pl.when(zs != z)
            def _():
                z_copy(zs, zs, k, right).wait_send()

        return carry

    lax.fori_loop(0, owners, settle, 0)


def solution(mesh):
    sizes = (mesh.shape["section"], mesh.shape["expert"], mesh.shape["tensor"])

    def local(slab, route_ids, route_weights, norm_gain, w_gate, w_up, w_down):
        owners = sizes[1]
        rows, width = slab.shape[1:]
        hidden = w_gate.shape[3]
        chunks = rows // CHUNK
        tall = 2 * rows
        vmem = pl.BlockSpec(memory_space=pltpu.VMEM)
        hbm = pl.BlockSpec(memory_space=pl.ANY)
        dma = pltpu.SemaphoreType.DMA
        flops = 2 * owners * tall * width * hidden * 2 * 3
        out = pl.pallas_call(
            functools.partial(kernel, sizes),
            out_shape=jax.ShapeDtypeStruct((rows, width), jnp.bfloat16),
            in_specs=[hbm, vmem, vmem, vmem, hbm, hbm, hbm],
            out_specs=vmem,
            scratch_shapes=[
                pltpu.VMEM((rows, width), jnp.bfloat16),
                pltpu.VMEM((owners, tall, width + PAD), jnp.bfloat16),
                pltpu.VMEM((CORES, width, hidden), jnp.bfloat16),
                pltpu.VMEM((CORES, width, hidden), jnp.bfloat16),
                pltpu.VMEM((CORES, hidden, width), jnp.bfloat16),
                pltpu.VMEM((tall, CORES * hidden), jnp.bfloat16),
                pltpu.VMEM((owners, tall, width), jnp.bfloat16),
                pltpu.VMEM((owners, rows, width), jnp.bfloat16),
                pltpu.VMEM((owners + 1, rows, width), jnp.bfloat16),
                dma((chunks,)),
                dma((chunks,)),
                dma((3,)),
                dma((3,)),
                dma((3,)),
                dma((owners, chunks)),
                dma((owners, chunks)),
                dma((owners, chunks)),
                dma((2, owners, chunks)),
                dma((owners, chunks)),
                dma((owners, chunks)),
                dma((owners, chunks)),
                dma((owners + 1, chunks)),
            ],
            compiler_params=pltpu.CompilerParams(
                collective_id=0,
                has_side_effects=True,
                vmem_limit_bytes=60 * 1024 * 1024,
            ),
            cost_estimate=pl.CostEstimate(
                flops=flops,
                bytes_accessed=12 * width * hidden,
                transcendentals=owners * tall * hidden * 2,
            ),
        )(
            slab[0],
            route_ids[0],
            route_weights[0],
            norm_gain,
            w_gate[0, 0],
            w_up[0, 0],
            w_down[0, 0],
        )
        return out[None]

    return jax.shard_map(
        local,
        mesh=mesh,
        in_specs=(
            P("section", ("expert", "tensor"), None),
            P("section", ("expert", "tensor"), None),
            P("section", ("expert", "tensor"), None),
            P("section", None),
            P("section", "expert", None, "tensor"),
            P("section", "expert", None, "tensor"),
            P("section", "expert", "tensor", None),
        ),
        out_specs=P("section", ("expert", "tensor"), None),
        check_vma=False,
    )
```

```python
import functools

import jax
import jax.numpy as jnp
from jax import lax
from jax.experimental import pallas as pl
from jax.experimental.pallas import tpu as pltpu
from jax.sharding import PartitionSpec as P

MESH = pl.DeviceIdType.MESH
CHUNK = 16
PAD = 128
CORES = 2


def kernel(
    sizes,
    slab_ref,
    dense_ref,
    gain_ref,
    wg_ref,
    wu_ref,
    wd_ref,
    out_ref,
    xbuf,
    tok,
    wgs,
    wus,
    wds,
    hid,
    part,
    yrecv,
    zrecv,
    x_send,
    x_recv,
    w_local,
    w_send,
    w_recv,
    t_right,
    t_left,
    t_y,
    t_recv,
    p_y,
    p_yrecv,
    p_z,
    p_zrecv,
    brecv,
    bown,
    b_right,
    b_left,
    b_recv,
    pb_z,
    pb_recv,
    last,
):
    sections, owners, groups = sizes
    rows, width = out_ref.shape
    chunks = rows // CHUNK
    first = yrecv.shape[2]
    section = lax.axis_index("section")
    z = lax.axis_index("expert")
    t = lax.axis_index("tensor")
    core = lax.rem(t, CORES)
    y = t // CORES
    other_y = 1 - y
    mate = {"tensor": y * CORES + 1 - core}
    across = {"tensor": other_y * CORES + core}
    ahead = {"section": lax.rem(section + 1, sections)}
    behind = {"section": lax.rem(section + sections - 1, sections)}
    right = {"expert": lax.rem(z + 1, owners)}
    left = {"expert": lax.rem(z + owners - 1, owners)}
    has_right = z < owners - 1
    has_left = z > 0

    def remote(src, dst, send, recv, where):
        return pltpu.make_async_remote_copy(
            src_ref=src,
            dst_ref=dst,
            send_sem=send,
            recv_sem=recv,
            device_id=where,
            device_id_type=MESH,
        )

    def lines(k, side=None):
        if side is None:
            return pl.ds(k * CHUNK, CHUNK)
        return pl.ds(pl.multiple_of(side * rows + k * CHUNK, CHUNK), CHUNK)

    barrier = pltpu.get_barrier_semaphore()
    for where in (mate, across, ahead, behind):
        pl.semaphore_signal(barrier, inc=1, device_id=where, device_id_type=MESH)

    @pl.when(has_right)
    def _():
        pl.semaphore_signal(barrier, inc=1, device_id=right, device_id_type=MESH)

    @pl.when(has_left)
    def _():
        pl.semaphore_signal(barrier, inc=1, device_id=left, device_id_type=MESH)

    edge = jnp.where(has_right, 1, 0) + jnp.where(has_left, 1, 0)
    pl.semaphore_wait(barrier, 4 + edge)

    def x_copy(k):
        return remote(
            slab_ref.at[lines(k)], xbuf.at[lines(k)], x_send.at[k], x_recv.at[k], ahead
        )

    for k in range(chunks):
        x_copy(k).start()

    weights = ((wg_ref, wgs), (wu_ref, wus), (wd_ref, wds))

    def w_copies(i):
        source, target = weights[i]
        return (
            pltpu.make_async_copy(source, target.at[core], w_local.at[i]),
            remote(source, target.at[core], w_send.at[i], w_recv.at[i], mate),
        )

    for i in range(3):
        for copy in w_copies(i):
            copy.start()

    def t_copy(zs, k, sends, where):
        place = tok.at[zs, lines(k, y)]
        return remote(place, place, sends.at[zs, k], t_recv.at[y, zs, k], where)

    def t_arrived(zs, side, k):
        place = tok.at[zs, lines(k, side)]
        return remote(place, place, t_y.at[zs, k], t_recv.at[side, zs, k], across)

    def a_copy(zs, side, k):
        place = tok.at[zs, lines(k, side), 0:first]
        return remote(place, place, t_y.at[zs, k], t_recv.at[side, zs, k], across)

    other_rows = pl.ds(pl.multiple_of(other_y * rows, CHUNK), rows)

    def b_copy(zs, sends, where):
        place = tok.at[zs, other_rows, first : width + PAD]
        return remote(place, place, sends.at[zs], b_recv.at[zs], where)

    def b_spread(zs, to_right, to_left):
        @pl.when(to_right)
        def _():
            b_copy(zs, b_right, right).start()

        @pl.when(to_left)
        def _():
            b_copy(zs, b_left, left).start()

    lane = lax.broadcasted_iota(jnp.int32, (CHUNK, PAD), 1)
    for k in range(chunks):
        x_copy(k).wait_recv()
        values = xbuf[lines(k)].astype(jnp.float32)
        scale = lax.rsqrt(jnp.mean(values * values, axis=-1, keepdims=True) + 1e-06)
        tok[z, lines(k, y), 0:width] = (values * scale * gain_ref[...]).astype(
            jnp.bfloat16
        )
        dense = dense_ref[lines(k)]
        high = dense.astype(jnp.bfloat16).astype(jnp.float32)
        rest = dense - high
        middle = rest.astype(jnp.bfloat16).astype(jnp.float32)
        low = rest - middle
        third = lane // owners
        packed = jnp.where(
            third == 0,
            high,
            jnp.where(third == 1, middle, jnp.where(third == 2, low, 0.0)),
        )
        tok[z, lines(k, y), width : width + PAD] = packed.astype(jnp.bfloat16)

        @pl.when(has_right)
        def _():
            t_copy(z, k, t_right, right).start()

        @pl.when(has_left)
        def _():
            t_copy(z, k, t_left, left).start()

        t_copy(z, k, t_y, across).start()

    for k in range(chunks):
        t_arrived(z, other_y, k).wait_recv()
    b_spread(z, has_right, has_left)

    def at(j):
        return z + ((j + 1) // 2) * (1 - 2 * lax.rem(j, 2))

    def inside(zs):
        return jnp.logical_and(zs >= 0, zs < owners)

    def forward(zs):
        for k in range(chunks):
            t_arrived(zs, y, k).wait_recv()

            @pl.when(jnp.logical_and(zs < z, has_right))
            def _():
                t_copy(zs, k, t_right, right).start()

            @pl.when(jnp.logical_and(zs > z, has_left))
            def _():
                t_copy(zs, k, t_left, left).start()

            a_copy(zs, y, k).start()
        b_copy(zs, b_right, right).wait_recv()
        b_spread(
            zs,
            jnp.logical_and(zs < z, has_right),
            jnp.logical_and(zs > z, has_left),
        )

    tall = 2 * rows
    hidden_width = wgs.shape[2]
    tile = width // 7 if width % (7 * 128) == 0 else 128

    def compute(zs):
        @pl.when(zs != z)
        def _():
            for k in range(chunks):
                a_copy(zs, other_y, k).wait_recv()

        for h in range(CORES):
            gate = jnp.dot(
                tok[zs, :, 0:width], wgs[h], preferred_element_type=jnp.float32
            )
            up = jnp.dot(
                tok[zs, :, 0:width], wus[h], preferred_element_type=jnp.float32
            )
            hid[:, h * hidden_width : (h + 1) * hidden_width] = (
                jax.nn.silu(gate) * up
            ).astype(jnp.bfloat16)
        spot = lax.broadcasted_iota(jnp.int32, (tall, PAD), 1)
        mine = jnp.logical_and(lax.rem(spot, owners) == z, spot < 3 * owners)
        share = jnp.sum(
            jnp.where(mine, tok[zs, :, width : width + PAD].astype(jnp.float32), 0.0),
            axis=1,
            keepdims=True,
        )

        def down(i, carry):
            span = pl.ds(pl.multiple_of(i * tile, 128), tile)
            product = jnp.dot(
                hid[:, 0:hidden_width],
                wds[0, :, span],
                preferred_element_type=jnp.float32,
            ) + jnp.dot(
                hid[:, hidden_width : 2 * hidden_width],
                wds[1, :, span],
                preferred_element_type=jnp.float32,
            )
            part[zs, :, span] = (product * share).astype(jnp.bfloat16)
            return carry

        lax.fori_loop(0, width // tile, down, 0)

    def gather_step(j, carry):
        zs = at(j)

        @pl.when(jnp.logical_and(j < 2 * owners - 1, inside(zs)))
        def _():
            forward(zs)

        before = at(j - 2)

        @pl.when(j == 2)
        def _():
            for i in range(3):
                local_copy, mate_copy = w_copies(i)
                local_copy.wait()
                remote(
                    weights[i][0],
                    weights[i][1].at[1 - core],
                    w_send.at[i],
                    w_recv.at[i],
                    mate,
                ).wait_recv()

        @pl.when(jnp.logical_and(j >= 2, inside(before)))
        def _():
            compute(before)

        return carry

    lax.fori_loop(1, 2 * owners + 1, gather_step, 0)

    def y_copy(zs, k):
        return remote(
            part.at[zs, lines(k, other_y), 0:first],
            yrecv.at[zs, lines(k)],
            p_y.at[zs, k],
            p_yrecv.at[zs, k],
            across,
        )

    def z_copy(zs, slot, k, where):
        return remote(
            part.at[zs, lines(k, y)],
            zrecv.at[slot, lines(k)],
            p_z.at[zs, k],
            p_zrecv.at[slot, k],
            where,
        )

    def c_copy(zs, slot, where):
        return remote(
            part.at[zs, other_rows, first:width],
            brecv.at[slot],
            pb_z.at[zs],
            pb_recv.at[slot],
            where,
        )

    def last_copy():
        return remote(
            part.at[z, other_rows, first:width],
            bown,
            last.at[0],
            last.at[1],
            across,
        )

    def send_y(i, carry):
        zs = at(2 * owners - 2 - i)

        @pl.when(inside(zs))
        def _():
            for k in range(chunks):
                y_copy(zs, k).start()

        return carry

    lax.fori_loop(0, 2 * owners - 1, send_y, 0)

    def reduce_step(i, carry):
        zs = at(2 * owners - 2 - i)

        @pl.when(inside(zs))
        def _():
            outer = jnp.logical_or(
                jnp.logical_and(zs > z, has_left),
                jnp.logical_and(zs < z, has_right),
            )
            slot = jnp.where(zs == z - 1, owners, zs)

            @pl.when(outer)
            def _():
                c_copy(zs, zs, right).wait_recv()
                part[zs, other_rows, first:width] = (
                    part[zs, other_rows, first:width].astype(jnp.float32)
                    + brecv[zs].astype(jnp.float32)
                ).astype(jnp.bfloat16)

            @pl.when(zs > z)
            def _():
                c_copy(zs, zs, right).start()

            @pl.when(zs < z)
            def _():
                c_copy(zs, slot, left).start()

            for k in range(chunks):
                y_copy(zs, k).wait_recv()
                here = lines(k, y)
                both = part[zs, here, 0:first].astype(jnp.float32) + yrecv[
                    zs, lines(k)
                ].astype(jnp.float32)

                @pl.when(outer)
                def _():
                    z_copy(zs, zs, k, right).wait_recv()
                    part[zs, here, 0:first] = (
                        both + zrecv[zs, lines(k), 0:first].astype(jnp.float32)
                    ).astype(jnp.bfloat16)
                    part[zs, here, first:width] = (
                        part[zs, here, first:width].astype(jnp.float32)
                        + zrecv[zs, lines(k), first:width].astype(jnp.float32)
                    ).astype(jnp.bfloat16)

                @pl.when(jnp.logical_not(outer))
                def _():
                    part[zs, here, 0:first] = both.astype(jnp.bfloat16)

                @pl.when(zs > z)
                def _():
                    z_copy(zs, zs, k, right).start()

                @pl.when(zs < z)
                def _():
                    z_copy(zs, slot, k, left).start()

        return carry

    lax.fori_loop(0, 2 * owners - 2, reduce_step, 0)

    @pl.when(has_left)
    def _():
        c_copy(z, z, right).wait_recv()

    @pl.when(jnp.logical_not(has_left))
    def _():
        brecv[z] = jnp.zeros(brecv.shape[1:], jnp.bfloat16)
        zrecv[z] = jnp.zeros(zrecv.shape[1:], jnp.bfloat16)

    @pl.when(has_right)
    def _():
        c_copy(z, owners, left).wait_recv()

    @pl.when(jnp.logical_not(has_right))
    def _():
        brecv[owners] = jnp.zeros(brecv.shape[1:], jnp.bfloat16)
        zrecv[owners] = jnp.zeros(zrecv.shape[1:], jnp.bfloat16)

    part[z, other_rows, first:width] = (
        part[z, other_rows, first:width].astype(jnp.float32)
        + brecv[z].astype(jnp.float32)
        + brecv[owners].astype(jnp.float32)
    ).astype(jnp.bfloat16)
    last_copy().start()

    def finish(k, span, extra):
        out_ref[lines(k), span] = (
            xbuf[lines(k), span].astype(jnp.float32)
            + part[z, lines(k, y), span].astype(jnp.float32)
            + zrecv[z, lines(k), span].astype(jnp.float32)
            + zrecv[owners, lines(k), span].astype(jnp.float32)
            + extra.astype(jnp.float32)
        ).astype(jnp.bfloat16)

    for k in range(chunks):
        y_copy(z, k).wait_recv()

        @pl.when(has_left)
        def _():
            z_copy(z, z, k, right).wait_recv()

        @pl.when(has_right)
        def _():
            z_copy(z, owners, k, left).wait_recv()

        finish(k, slice(0, first), yrecv[z, lines(k)])
    last_copy().wait_recv()
    for k in range(chunks):
        finish(k, slice(first, width), bown[lines(k)])

    for k in range(chunks):
        x_copy(k).wait_send()
    for i in range(3):
        w_copies(i)[1].wait_send()
    last_copy().wait_send()
    for k in range(chunks):
        t_copy(z, k, t_y, across).wait_send()

    def settle(zs, carry):
        @pl.when(jnp.logical_and(zs <= z, has_right))
        def _():
            b_copy(zs, b_right, right).wait_send()

        @pl.when(jnp.logical_and(zs >= z, has_left))
        def _():
            b_copy(zs, b_left, left).wait_send()

        @pl.when(zs != z)
        def _():
            c_copy(zs, zs, right).wait_send()
            for k in range(chunks):
                a_copy(zs, y, k).wait_send()

        for k in range(chunks):
            y_copy(zs, k).wait_send()

            @pl.when(jnp.logical_and(zs <= z, has_right))
            def _():
                t_copy(zs, k, t_right, right).wait_send()

            @pl.when(jnp.logical_and(zs >= z, has_left))
            def _():
                t_copy(zs, k, t_left, left).wait_send()

            @pl.when(zs != z)
            def _():
                z_copy(zs, zs, k, right).wait_send()

        return carry

    lax.fori_loop(0, owners, settle, 0)


def solution(mesh):
    sizes = (mesh.shape["section"], mesh.shape["expert"], mesh.shape["tensor"])

    def local(slab, route_ids, route_weights, norm_gain, w_gate, w_up, w_down):
        owners = sizes[1]
        rows, width = slab.shape[1:]
        hidden = w_gate.shape[3]
        chunks = rows // CHUNK
        tall = 2 * rows
        tiles = width // 128
        beyond = 128 * max(1, tiles // (2 * (owners - 1)))
        column = jnp.arange(PAD, dtype=jnp.int32) % owners
        dense = jnp.sum(
            jnp.where(
                route_ids[0][:, :, None] == column[None, None, :],
                route_weights[0][:, :, None],
                0.0,
            ),
            axis=1,
        )
        vmem = pl.BlockSpec(memory_space=pltpu.VMEM)
        hbm = pl.BlockSpec(memory_space=pl.ANY)
        dma = pltpu.SemaphoreType.DMA
        flops = 2 * owners * tall * width * hidden * 2 * 3
        out = pl.pallas_call(
            functools.partial(kernel, sizes),
            out_shape=jax.ShapeDtypeStruct((rows, width), jnp.bfloat16),
            in_specs=[hbm, vmem, vmem, hbm, hbm, hbm],
            out_specs=vmem,
            scratch_shapes=[
                pltpu.VMEM((rows, width), jnp.bfloat16),
                pltpu.VMEM((owners, tall, width + PAD), jnp.bfloat16),
                pltpu.VMEM((CORES, width, hidden), jnp.bfloat16),
                pltpu.VMEM((CORES, width, hidden), jnp.bfloat16),
                pltpu.VMEM((CORES, hidden, width), jnp.bfloat16),
                pltpu.VMEM((tall, CORES * hidden), jnp.bfloat16),
                pltpu.VMEM((owners, tall, width), jnp.bfloat16),
                pltpu.VMEM((owners, rows, width - beyond), jnp.bfloat16),
                pltpu.VMEM((owners + 1, rows, width), jnp.bfloat16),
                dma((chunks,)),
                dma((chunks,)),
                dma((3,)),
                dma((3,)),
                dma((3,)),
                dma((owners, chunks)),
                dma((owners, chunks)),
                dma((owners, chunks)),
                dma((2, owners, chunks)),
                dma((owners, chunks)),
                dma((owners, chunks)),
                dma((owners, chunks)),
                dma((owners + 1, chunks)),
                pltpu.VMEM((owners + 1, rows, beyond), jnp.bfloat16),
                pltpu.VMEM((rows, beyond), jnp.bfloat16),
                dma((owners,)),
                dma((owners,)),
                dma((owners,)),
                dma((owners,)),
                dma((owners + 1,)),
                dma((2,)),
            ],
            compiler_params=pltpu.CompilerParams(
                collective_id=0,
                has_side_effects=True,
                vmem_limit_bytes=60 * 1024 * 1024,
            ),
            cost_estimate=pl.CostEstimate(
                flops=flops,
                bytes_accessed=12 * width * hidden,
                transcendentals=owners * tall * hidden * 2,
            ),
        )(
            slab[0],
            dense,
            norm_gain,
            w_gate[0, 0],
            w_up[0, 0],
            w_down[0, 0],
        )
        return out[None]

    return jax.shard_map(
        local,
        mesh=mesh,
        in_specs=(
            P("section", ("expert", "tensor"), None),
            P("section", ("expert", "tensor"), None),
            P("section", ("expert", "tensor"), None),
            P("section", None),
            P("section", "expert", None, "tensor"),
            P("section", "expert", None, "tensor"),
            P("section", "expert", "tensor", None),
        ),
        out_specs=P("section", ("expert", "tensor"), None),
        check_vma=False,
    )
```

```python
import functools

import jax
import jax.numpy as jnp
from jax import lax
from jax.experimental import pallas as pl
from jax.experimental.pallas import tpu as pltpu
from jax.sharding import PartitionSpec as P

MESH = pl.DeviceIdType.MESH
CHUNK = 16
PAD = 128
CORES = 2


def kernel(
    sizes,
    slab_ref,
    dense_ref,
    gain_ref,
    wg_ref,
    wu_ref,
    wd_ref,
    out_ref,
    xbuf,
    tok,
    wgs,
    wus,
    wds,
    hid,
    part,
    yrecv,
    zrecv,
    x_send,
    x_recv,
    w_local,
    w_send,
    w_recv,
    t_right,
    t_left,
    t_y,
    t_recv,
    p_y,
    p_yrecv,
    p_z,
    p_zrecv,
    brecv,
    bown,
    b_right,
    b_left,
    b_recv,
    pb_z,
    pb_recv,
    last,
):
    sections, owners, groups = sizes
    rows, width = out_ref.shape
    chunks = rows // CHUNK
    first = yrecv.shape[2]
    section = lax.axis_index("section")
    z = lax.axis_index("expert")
    t = lax.axis_index("tensor")
    core = lax.rem(t, CORES)
    y = t // CORES
    other_y = 1 - y
    mate = {"tensor": y * CORES + 1 - core}
    across = {"tensor": other_y * CORES + core}
    ahead = {"section": lax.rem(section + 1, sections)}
    behind = {"section": lax.rem(section + sections - 1, sections)}
    right = {"expert": lax.rem(z + 1, owners)}
    left = {"expert": lax.rem(z + owners - 1, owners)}
    has_right = z < owners - 1
    has_left = z > 0

    def remote(src, dst, send, recv, where):
        return pltpu.make_async_remote_copy(
            src_ref=src,
            dst_ref=dst,
            send_sem=send,
            recv_sem=recv,
            device_id=where,
            device_id_type=MESH,
        )

    def lines(k, side=None):
        if side is None:
            return pl.ds(k * CHUNK, CHUNK)
        return pl.ds(pl.multiple_of(side * rows + k * CHUNK, CHUNK), CHUNK)

    barrier = pltpu.get_barrier_semaphore()
    for where in (mate, across, ahead, behind):
        pl.semaphore_signal(barrier, inc=1, device_id=where, device_id_type=MESH)

    @pl.when(has_right)
    def _():
        pl.semaphore_signal(barrier, inc=1, device_id=right, device_id_type=MESH)

    @pl.when(has_left)
    def _():
        pl.semaphore_signal(barrier, inc=1, device_id=left, device_id_type=MESH)

    edge = jnp.where(has_right, 1, 0) + jnp.where(has_left, 1, 0)
    pl.semaphore_wait(barrier, 4 + edge)

    def x_copy(k):
        return remote(
            slab_ref.at[lines(k)], xbuf.at[lines(k)], x_send.at[k], x_recv.at[k], ahead
        )

    for k in range(chunks):
        x_copy(k).start()

    weights = ((wg_ref, wgs), (wu_ref, wus), (wd_ref, wds))

    def w_copies(i):
        source, target = weights[i]
        return (
            pltpu.make_async_copy(source, target.at[core], w_local.at[i]),
            remote(source, target.at[core], w_send.at[i], w_recv.at[i], mate),
        )

    for i in range(3):
        for copy in w_copies(i):
            copy.start()

    def t_copy(zs, k, sends, where):
        place = tok.at[zs, lines(k, y)]
        return remote(place, place, sends.at[zs, k], t_recv.at[y, zs, k], where)

    def t_arrived(zs, side, k):
        place = tok.at[zs, lines(k, side)]
        return remote(place, place, t_y.at[zs, k], t_recv.at[side, zs, k], across)

    def a_copy(zs, side, k):
        place = tok.at[zs, lines(k, side), 0:first]
        return remote(place, place, t_y.at[zs, k], t_recv.at[side, zs, k], across)

    other_rows = pl.ds(pl.multiple_of(other_y * rows, CHUNK), rows)

    def b_copy(zs, sends, where):
        place = tok.at[zs, other_rows, first : width + PAD]
        return remote(place, place, sends.at[zs], b_recv.at[zs], where)

    def b_spread(zs, to_right, to_left):
        @pl.when(to_right)
        def _():
            b_copy(zs, b_right, right).start()

        @pl.when(to_left)
        def _():
            b_copy(zs, b_left, left).start()

    lane = lax.broadcasted_iota(jnp.int32, (CHUNK, PAD), 1)
    for k in range(chunks):
        x_copy(k).wait_recv()
        values = xbuf[lines(k)].astype(jnp.float32)
        scale = lax.rsqrt(jnp.mean(values * values, axis=-1, keepdims=True) + 1e-06)
        tok[z, lines(k, y), 0:width] = (values * scale * gain_ref[...]).astype(
            jnp.bfloat16
        )
        dense = dense_ref[lines(k)]
        high = dense.astype(jnp.bfloat16).astype(jnp.float32)
        rest = dense - high
        middle = rest.astype(jnp.bfloat16).astype(jnp.float32)
        low = rest - middle
        third = lane // owners
        packed = jnp.where(
            third == 0,
            high,
            jnp.where(third == 1, middle, jnp.where(third == 2, low, 0.0)),
        )
        tok[z, lines(k, y), width : width + PAD] = packed.astype(jnp.bfloat16)

        @pl.when(has_right)
        def _():
            t_copy(z, k, t_right, right).start()

        @pl.when(has_left)
        def _():
            t_copy(z, k, t_left, left).start()

        t_copy(z, k, t_y, across).start()

    for k in range(chunks):
        t_arrived(z, other_y, k).wait_recv()
    b_spread(z, has_right, has_left)

    near = 1 - 2 * ((2 * z) // owners)

    def at(j):
        return z + ((j + 1) // 2) * (1 - 2 * lax.rem(j, 2)) * near

    def outside_in(i):
        return z - (owners - 1 - i // 2) * (1 - 2 * lax.rem(i, 2)) * near

    def inside(zs):
        return jnp.logical_and(zs >= 0, zs < owners)

    def forward(sides):
        for k in range(chunks):
            for zs in sides:

                @pl.when(inside(zs))
                def _():
                    t_arrived(zs, y, k).wait_recv()

                    @pl.when(jnp.logical_and(zs < z, has_right))
                    def _():
                        t_copy(zs, k, t_right, right).start()

                    @pl.when(jnp.logical_and(zs > z, has_left))
                    def _():
                        t_copy(zs, k, t_left, left).start()

                    a_copy(zs, y, k).start()

        for zs in sides:

            @pl.when(inside(zs))
            def _():
                b_copy(zs, b_right, right).wait_recv()
                b_spread(
                    zs,
                    jnp.logical_and(zs < z, has_right),
                    jnp.logical_and(zs > z, has_left),
                )

    tall = 2 * rows
    hidden_width = wgs.shape[2]
    tile = width // 7 if width % (7 * 128) == 0 else 128

    def compute(zs):
        @pl.when(zs != z)
        def _():
            for k in range(chunks):
                a_copy(zs, other_y, k).wait_recv()

        for h in range(CORES):
            gate = jnp.dot(
                tok[zs, :, 0:width], wgs[h], preferred_element_type=jnp.float32
            )
            up = jnp.dot(
                tok[zs, :, 0:width], wus[h], preferred_element_type=jnp.float32
            )
            hid[:, h * hidden_width : (h + 1) * hidden_width] = (
                jax.nn.silu(gate) * up
            ).astype(jnp.bfloat16)
        spot = lax.broadcasted_iota(jnp.int32, (tall, PAD), 1)
        mine = jnp.logical_and(lax.rem(spot, owners) == z, spot < 3 * owners)
        share = jnp.sum(
            jnp.where(mine, tok[zs, :, width : width + PAD].astype(jnp.float32), 0.0),
            axis=1,
            keepdims=True,
        )

        def down(i, carry):
            span = pl.ds(pl.multiple_of(i * tile, 128), tile)
            product = jnp.dot(
                hid[:, 0:hidden_width],
                wds[0, :, span],
                preferred_element_type=jnp.float32,
            ) + jnp.dot(
                hid[:, hidden_width : 2 * hidden_width],
                wds[1, :, span],
                preferred_element_type=jnp.float32,
            )
            part[zs, :, span] = (product * share).astype(jnp.bfloat16)
            return carry

        lax.fori_loop(0, width // tile, down, 0)

    def gather_step(j, carry):
        @pl.when(jnp.logical_and(lax.rem(j, 2) == 1, j < 2 * owners - 1))
        def _():
            forward((at(j), at(j + 1)))

        before = at(j - 2)

        @pl.when(j == 2)
        def _():
            for i in range(3):
                local_copy, mate_copy = w_copies(i)
                local_copy.wait()
                remote(
                    weights[i][0],
                    weights[i][1].at[1 - core],
                    w_send.at[i],
                    w_recv.at[i],
                    mate,
                ).wait_recv()

        @pl.when(jnp.logical_and(j >= 2, inside(before)))
        def _():
            compute(before)

        return carry

    lax.fori_loop(1, 2 * owners + 1, gather_step, 0)

    def y_copy(zs, k):
        return remote(
            part.at[zs, lines(k, other_y), 0:first],
            yrecv.at[zs, lines(k)],
            p_y.at[zs, k],
            p_yrecv.at[zs, k],
            across,
        )

    def z_copy(zs, slot, k, where):
        return remote(
            part.at[zs, lines(k, y)],
            zrecv.at[slot, lines(k)],
            p_z.at[zs, k],
            p_zrecv.at[slot, k],
            where,
        )

    def c_copy(zs, slot, where):
        return remote(
            part.at[zs, other_rows, first:width],
            brecv.at[slot],
            pb_z.at[zs],
            pb_recv.at[slot],
            where,
        )

    def last_copy():
        return remote(
            part.at[z, other_rows, first:width],
            bown,
            last.at[0],
            last.at[1],
            across,
        )

    def send_y(i, carry):
        zs = outside_in(i)

        @pl.when(inside(zs))
        def _():
            for k in range(chunks):
                y_copy(zs, k).start()

        return carry

    lax.fori_loop(0, 2 * owners - 1, send_y, 0)

    def reduce_step(i, carry):
        zs = outside_in(i)

        @pl.when(inside(zs))
        def _():
            outer = jnp.logical_or(
                jnp.logical_and(zs > z, has_left),
                jnp.logical_and(zs < z, has_right),
            )
            slot = jnp.where(zs == z - 1, owners, zs)

            @pl.when(outer)
            def _():
                c_copy(zs, zs, right).wait_recv()
                part[zs, other_rows, first:width] = (
                    part[zs, other_rows, first:width].astype(jnp.float32)
                    + brecv[zs].astype(jnp.float32)
                ).astype(jnp.bfloat16)

            @pl.when(zs > z)
            def _():
                c_copy(zs, zs, right).start()

            @pl.when(zs < z)
            def _():
                c_copy(zs, slot, left).start()

            for k in range(chunks):
                y_copy(zs, k).wait_recv()
                here = lines(k, y)
                both = part[zs, here, 0:first].astype(jnp.float32) + yrecv[
                    zs, lines(k)
                ].astype(jnp.float32)

                @pl.when(outer)
                def _():
                    z_copy(zs, zs, k, right).wait_recv()
                    part[zs, here, 0:first] = (
                        both + zrecv[zs, lines(k), 0:first].astype(jnp.float32)
                    ).astype(jnp.bfloat16)
                    part[zs, here, first:width] = (
                        part[zs, here, first:width].astype(jnp.float32)
                        + zrecv[zs, lines(k), first:width].astype(jnp.float32)
                    ).astype(jnp.bfloat16)

                @pl.when(jnp.logical_not(outer))
                def _():
                    part[zs, here, 0:first] = both.astype(jnp.bfloat16)

                @pl.when(zs > z)
                def _():
                    z_copy(zs, zs, k, right).start()

                @pl.when(zs < z)
                def _():
                    z_copy(zs, slot, k, left).start()

        return carry

    lax.fori_loop(0, 2 * owners - 2, reduce_step, 0)

    @pl.when(has_left)
    def _():
        c_copy(z, z, right).wait_recv()

    @pl.when(jnp.logical_not(has_left))
    def _():
        brecv[z] = jnp.zeros(brecv.shape[1:], jnp.bfloat16)
        zrecv[z] = jnp.zeros(zrecv.shape[1:], jnp.bfloat16)

    @pl.when(has_right)
    def _():
        c_copy(z, owners, left).wait_recv()

    @pl.when(jnp.logical_not(has_right))
    def _():
        brecv[owners] = jnp.zeros(brecv.shape[1:], jnp.bfloat16)
        zrecv[owners] = jnp.zeros(zrecv.shape[1:], jnp.bfloat16)

    part[z, other_rows, first:width] = (
        part[z, other_rows, first:width].astype(jnp.float32)
        + brecv[z].astype(jnp.float32)
        + brecv[owners].astype(jnp.float32)
    ).astype(jnp.bfloat16)
    last_copy().start()

    def finish(k, span, extra):
        out_ref[lines(k), span] = (
            xbuf[lines(k), span].astype(jnp.float32)
            + part[z, lines(k, y), span].astype(jnp.float32)
            + zrecv[z, lines(k), span].astype(jnp.float32)
            + zrecv[owners, lines(k), span].astype(jnp.float32)
            + extra.astype(jnp.float32)
        ).astype(jnp.bfloat16)

    for k in range(chunks):
        y_copy(z, k).wait_recv()

        @pl.when(has_left)
        def _():
            z_copy(z, z, k, right).wait_recv()

        @pl.when(has_right)
        def _():
            z_copy(z, owners, k, left).wait_recv()

        finish(k, slice(0, first), yrecv[z, lines(k)])
    last_copy().wait_recv()
    for k in range(chunks):
        finish(k, slice(first, width), bown[lines(k)])

    for k in range(chunks):
        x_copy(k).wait_send()
    for i in range(3):
        w_copies(i)[1].wait_send()
    last_copy().wait_send()
    for k in range(chunks):
        t_copy(z, k, t_y, across).wait_send()

    def settle(zs, carry):
        @pl.when(jnp.logical_and(zs <= z, has_right))
        def _():
            b_copy(zs, b_right, right).wait_send()

        @pl.when(jnp.logical_and(zs >= z, has_left))
        def _():
            b_copy(zs, b_left, left).wait_send()

        @pl.when(zs != z)
        def _():
            c_copy(zs, zs, right).wait_send()
            for k in range(chunks):
                a_copy(zs, y, k).wait_send()

        for k in range(chunks):
            y_copy(zs, k).wait_send()

            @pl.when(jnp.logical_and(zs <= z, has_right))
            def _():
                t_copy(zs, k, t_right, right).wait_send()

            @pl.when(jnp.logical_and(zs >= z, has_left))
            def _():
                t_copy(zs, k, t_left, left).wait_send()

            @pl.when(zs != z)
            def _():
                z_copy(zs, zs, k, right).wait_send()

        return carry

    lax.fori_loop(0, owners, settle, 0)


def solution(mesh):
    sizes = (mesh.shape["section"], mesh.shape["expert"], mesh.shape["tensor"])

    def local(slab, route_ids, route_weights, norm_gain, w_gate, w_up, w_down):
        owners = sizes[1]
        rows, width = slab.shape[1:]
        hidden = w_gate.shape[3]
        chunks = rows // CHUNK
        tall = 2 * rows
        tiles = width // 128
        beyond = 128 * max(1, tiles // (2 * owners))
        column = jnp.arange(PAD, dtype=jnp.int32) % owners
        dense = jnp.sum(
            jnp.where(
                route_ids[0][:, :, None] == column[None, None, :],
                route_weights[0][:, :, None],
                0.0,
            ),
            axis=1,
        )
        vmem = pl.BlockSpec(memory_space=pltpu.VMEM)
        hbm = pl.BlockSpec(memory_space=pl.ANY)
        dma = pltpu.SemaphoreType.DMA
        flops = 2 * owners * tall * width * hidden * 2 * 3
        out = pl.pallas_call(
            functools.partial(kernel, sizes),
            out_shape=jax.ShapeDtypeStruct((rows, width), jnp.bfloat16),
            in_specs=[hbm, vmem, vmem, hbm, hbm, hbm],
            out_specs=vmem,
            scratch_shapes=[
                pltpu.VMEM((rows, width), jnp.bfloat16),
                pltpu.VMEM((owners, tall, width + PAD), jnp.bfloat16),
                pltpu.VMEM((CORES, width, hidden), jnp.bfloat16),
                pltpu.VMEM((CORES, width, hidden), jnp.bfloat16),
                pltpu.VMEM((CORES, hidden, width), jnp.bfloat16),
                pltpu.VMEM((tall, CORES * hidden), jnp.bfloat16),
                pltpu.VMEM((owners, tall, width), jnp.bfloat16),
                pltpu.VMEM((owners, rows, width - beyond), jnp.bfloat16),
                pltpu.VMEM((owners + 1, rows, width), jnp.bfloat16),
                dma((chunks,)),
                dma((chunks,)),
                dma((3,)),
                dma((3,)),
                dma((3,)),
                dma((owners, chunks)),
                dma((owners, chunks)),
                dma((owners, chunks)),
                dma((2, owners, chunks)),
                dma((owners, chunks)),
                dma((owners, chunks)),
                dma((owners, chunks)),
                dma((owners + 1, chunks)),
                pltpu.VMEM((owners + 1, rows, beyond), jnp.bfloat16),
                pltpu.VMEM((rows, beyond), jnp.bfloat16),
                dma((owners,)),
                dma((owners,)),
                dma((owners,)),
                dma((owners,)),
                dma((owners + 1,)),
                dma((2,)),
            ],
            compiler_params=pltpu.CompilerParams(
                collective_id=0,
                has_side_effects=True,
                vmem_limit_bytes=60 * 1024 * 1024,
            ),
            cost_estimate=pl.CostEstimate(
                flops=flops,
                bytes_accessed=12 * width * hidden,
                transcendentals=owners * tall * hidden * 2,
            ),
        )(
            slab[0],
            dense,
            norm_gain,
            w_gate[0, 0],
            w_up[0, 0],
            w_down[0, 0],
        )
        return out[None]

    return jax.shard_map(
        local,
        mesh=mesh,
        in_specs=(
            P("section", ("expert", "tensor"), None),
            P("section", ("expert", "tensor"), None),
            P("section", ("expert", "tensor"), None),
            P("section", None),
            P("section", "expert", None, "tensor"),
            P("section", "expert", None, "tensor"),
            P("section", "expert", "tensor", None),
        ),
        out_specs=P("section", ("expert", "tensor"), None),
        check_vma=False,
    )
```
